32 devices in a mesh: row: 4 (over z), col: 2 (over x), sub: 4 (over y, core).
Axes of the slice: x: 2, y: 2, z: 4, core: 2. Of those that a mesh axis runs over, the one named last changes fastest.
Arguments:
- front_entries: float32 [8192, 8192], P('row', ('col', 'sub')), may hold values from -1 to 4, as said below
- child_blocks: float32 [4, 2048, 2048], P('sub', 'row', 'col'), may hold values from -1 to 2, as said below
- child_map: int32 [4, 16], P('sub'), may hold values from 0 to 63, as said below
Outputs:
- factored: float32 [8192, 8192], P('row', ('col', 'sub'))
The draws below stay inside these ranges and needn't reach their ends.
Inputs may be any that keep to these rules, and one draw needn't show every extreme that they name: Each row of child_map lists 16 different parent blocks in increasing order and ends with block 63. In natural order front_entries is a symmetric matrix, and the assembled front is positive definite. `child_blocks`: in natural order each child's contribution block is a symmetric matrix.
All inputs are finite; a program needn't handle non-finite values.
Results may differ from the reference program's by a relative error of at most 0.00005.
Values sent between devices are 32-bit elements; how exact they have to be, the bound alone decides.
No kernel may reach another device: no remote copies, remote signals or barrier semaphores. Data moves between devices by JAX's collectives and lax.ppermute only.
A program may use at most 192 MiB of HBM per device.

```python
import math
import jax
import jax.numpy as jnp
from jax import lax

BLK = 128
FB = 64
CBB = 16
NPIV = 6
NCHILD = 4
F = 8192
CB = 2048
N_ROW = 4
N_COL = 2


def natural_positions(order, groups):
    span = order // BLK // groups
    position = jnp.arange(order, dtype=jnp.int32)
    block = position // BLK
    return ((block % span * groups + block // span) * BLK + position % BLK).astype(jnp.int32)


def kernel_draw(key, order, noise_norm, diag_low, diag_high, amplitude):
    point_key, noise_key, diag_key = jax.random.split(key, 3)
    points = jax.random.uniform(point_key, (order,), jnp.float32, 0.0, order / 4.0)
    kernel = amplitude * jnp.exp(-jnp.abs(points[:, None] - points[None, :]))
    spread = noise_norm / (2.0 * math.sqrt(order))
    noise_field = jax.random.normal(noise_key, (order, order), jnp.float32) * spread
    diagonal = jax.random.uniform(diag_key, (order,), jnp.float32, diag_low, diag_high)
    symmetric = (noise_field + noise_field.T) * 0.7071
    return kernel + symmetric + jnp.diag(diagonal)


def draw_front_entries(key, part):
    matrix = kernel_draw(jax.random.fold_in(key, 11), F, 0.5, 1.0, 2.0, 1.0)
    row_places = natural_positions(F, N_ROW)
    col_places = natural_positions(F, N_COL)
    return matrix[row_places][:, col_places]


def draw_child_blocks(key, part):
    child_keys = jax.random.split(jax.random.fold_in(key, 23), NCHILD)
    row_places = natural_positions(CB, N_ROW)
    col_places = natural_positions(CB, N_COL)

    def draw_one_child(child_key):
        matrix = kernel_draw(child_key, CB, 0.25, 0.5, 1.0, 0.5)
        return matrix[row_places][:, col_places]
    return jax.vmap(draw_one_child)(child_keys)


def draw_child_map(key, part):
    child_keys = jax.random.split(jax.random.fold_in(key, 37), NCHILD)

    def draw_one_list(child_key):
        shuffled = jax.random.permutation(child_key, FB - 1).astype(jnp.int32)
        chosen = jnp.sort(shuffled[:CBB - 1])
        return jnp.concatenate([chosen, jnp.full((1,), FB - 1, jnp.int32)]).astype(jnp.int32)
    return jax.vmap(draw_one_list)(child_keys)


def setup_inputs(seed: int = 0) -> dict:
    arg_keys = jax.random.split(jax.random.key(seed), 4)
    front_entries = draw_front_entries(jax.random.fold_in(arg_keys[3], 71), 0)
    child_blocks = draw_child_blocks(jax.random.fold_in(arg_keys[3], 71), 0)
    child_map = draw_child_map(jax.random.fold_in(arg_keys[3], 71), 0)
    return dict(front_entries=front_entries, child_blocks=child_blocks, child_map=child_map)


def natural(stored, row_groups, col_groups):
    row_total, col_total = stored.shape
    row_span = row_total // BLK // row_groups
    col_span = col_total // BLK // col_groups
    reordered = stored.reshape(row_groups, row_span, BLK, col_total).transpose(1, 0, 2, 3).reshape(row_total, col_total)
    return reordered.reshape(row_total, col_groups, col_span, BLK).transpose(0, 2, 1, 3).reshape(row_total, col_total)

def stored_order(matrix, row_groups, col_groups):
    row_total, col_total = matrix.shape
    row_span = row_total // BLK // row_groups
    col_span = col_total // BLK // col_groups
    reordered = matrix.reshape(row_span, row_groups, BLK, col_total).transpose(1, 0, 2, 3).reshape(row_total, col_total)
    return reordered.reshape(row_total, col_span, col_groups, BLK).transpose(0, 2, 1, 3).reshape(row_total, col_total)

def reference(front_entries, child_blocks, child_map):
    assembled = natural(front_entries, N_ROW, N_COL)
    within = jnp.arange(BLK, dtype=jnp.int32)
    for child_number in range(NCHILD):
        child_natural = natural(child_blocks[child_number], N_ROW, N_COL)
        index_list = (child_map[child_number][:, None] * BLK + within[None, :]).reshape(-1).astype(jnp.int32)
        assembled = assembled.at[index_list[:, None], index_list[None, :]].add(child_natural)
    pivots = NPIV * BLK
    leading = jnp.linalg.cholesky(assembled[:pivots, :pivots])
    lower_left = jax.scipy.linalg.solve_triangular(leading, assembled[pivots:, :pivots].T, lower=True).T
    schur_block = assembled[pivots:, pivots:] - jnp.dot(lower_left, lower_left.T, precision=lax.Precision.HIGHEST)
    upper_half = jnp.concatenate([leading, jnp.zeros((pivots, F - pivots), jnp.float32)], axis=1)
    bottom = jnp.concatenate([lower_left, schur_block], axis=1)
    return stored_order(jnp.concatenate([upper_half, bottom], axis=0), N_ROW, N_COL)
```

```python
import functools

import jax
import jax.numpy as jnp
from jax import lax
from jax.experimental import pallas as pl
from jax.experimental.pallas import tpu as pltpu
from jax.sharding import PartitionSpec as P

BLK = 128
NPIV = 6
PLANE = ("col", "sub")
VMEM_BYTES = 60 * 1024 * 1024

highest = lax.Precision.HIGHEST


def quot(value, number):
    if number & (number - 1) == 0:
        return lax.shift_right_logical(value, jnp.int32(number.bit_length() - 1))
    return lax.div(value, jnp.int32(number))


def rem(value, number):
    if number & (number - 1) == 0:
        return value & (number - 1)
    return lax.rem(value, jnp.int32(number))


def whole(memory):
    return pl.BlockSpec(memory_space=memory)


def params(**more):
    return pltpu.CompilerParams(vmem_limit_bytes=VMEM_BYTES, **more)


class Plan:
    def __init__(self, front_shape, child_shape):
        self.rows = lax.axis_size("row")
        self.cols = lax.axis_size("col")
        self.subs = lax.axis_size("sub")
        self.plane = self.cols * self.subs
        self.part = BLK // self.plane
        self.row_blocks = front_shape[0] // BLK
        self.slots = front_shape[1] // BLK
        self.child_rows = child_shape[1] // BLK
        self.child_cols = child_shape[2] // BLK
        self.order = self.child_rows * self.rows
        self.lead_cols = -(-NPIV // self.cols)
        self.lead_rows = -(-NPIV // self.rows)
        reach = [
            min((self.rows * t + self.rows - 1) // self.cols + 1, self.child_cols)
            for t in range(self.child_rows)
        ]
        first = [(t, u) for t in range(self.child_rows) for u in range(min(reach[t], self.lead_cols))]
        second = [(t, u) for t in range(self.child_rows) for u in range(self.lead_cols, reach[t])]
        self.first = len(first)
        self.second = len(second)
        self.blocks = first + second
        self.first_start = [first.index((t, 0)) for t in range(self.child_rows)]
        self.second_start = [
            sum(1 for b in second if b[0] < t) for t in range(self.child_rows)
        ]

    def dest(self, block):
        high = quot(block, self.cols)
        return rem(block, self.cols), quot(high, self.slots), rem(high, self.slots)

    def offset(self, starts, t):
        out = jnp.int32(starts[0])
        for step in range(1, len(starts)):
            out = jnp.where(t == step, jnp.int32(starts[step]), out)
        return out


def take_rows(ref, lead, base, index, part, lanes):
    if part % 8 == 0:
        return ref[(*lead, pl.ds(pl.multiple_of(base + index * part, part), part), lanes)]
    share = 8 // part
    group = ref[(*lead, pl.ds(pl.multiple_of(base + quot(index, share) * 8, 8), 8), lanes)]
    out = group[:part]
    for step in range(1, share):
        out = jnp.where(rem(index, share) == step, group[step * part : (step + 1) * part], out)
    return out


def put_rows(ref, base, index, lanes, value):
    part = value.shape[0]
    if part % 8 == 0:
        ref[pl.ds(pl.multiple_of(base + index * part, part), part), lanes] = value
        return
    share = 8 // part
    rows = pl.ds(pl.multiple_of(base + quot(index, share) * 8, 8), 8)
    spot = lax.broadcasted_iota(jnp.int32, (8, value.shape[1]), 0)
    mine = quot(spot, part) == rem(index, share)
    ref[rows, lanes] = jnp.where(mine, jnp.concatenate([value] * share, axis=0), ref[rows, lanes])


def block_lanes(number):
    return slice(number * BLK, (number + 1) * BLK)


def cut_child_kernel(plan, place_ref, tile_ref, *out_refs):
    me = place_ref[0]
    for m, out_ref in enumerate(out_refs):
        for b, (t, u) in enumerate(plan.blocks):
            out_ref[b] = take_rows(tile_ref, (0,), t * BLK, me ^ m, plan.part, block_lanes(u))


def cut_front_kernel(plan, place_ref, front_ref, *out_refs):
    me = place_ref[0]

    @pl.loop(0, plan.row_blocks)
    def _(t):
        for m, out_ref in enumerate(out_refs):
            for u in range(plan.lead_cols):
                out_ref[t, u] = take_rows(front_ref, (), t * BLK, me ^ m, plan.part, block_lanes(u))


def front_panel_kernel(plan, place_ref, *refs):
    pieces = refs[: plan.plane]
    panel_ref, lead_ref = refs[plan.plane :]
    col, sub = place_ref[2], place_ref[3]
    panel_ref[...] = jnp.zeros_like(panel_ref)
    for mc in range(plan.cols):
        for u in range(plan.lead_cols):
            pivot = plan.cols * u + (col ^ mc)

            @pl.when(pivot < NPIV)
            def _():
                @pl.loop(0, plan.row_blocks)
                def _(t):
                    total = jnp.zeros((plan.part, BLK), jnp.float32)
                    for ms in range(plan.subs):
                        piece = pieces[mc * plan.subs + ms][t, u]
                        if mc == 0 and ms == 0:
                            piece = jnp.where(sub == 0, piece, 0.0)
                        total = total + piece
                    panel_ref[t, pivot] = total

    lead_ref[...] = panel_ref[: plan.lead_rows]


def panel_kernel(plan, place_ref, maps_ref, *refs):
    rows = plan.rows
    ring = refs[:rows]
    leads = refs[rows : 2 * rows]
    front_ref = refs[2 * rows]
    panel_ref, corner_ref = refs[2 * rows + 1 : 2 * rows + 3]
    outs = refs[2 * rows + 3 : 2 * rows + 3 + plan.plane]
    held, across, sems = refs[2 * rows + 3 + plan.plane :]
    row, col, sub = place_ref[1], place_ref[2], place_ref[3]
    copies = [
        pltpu.make_async_copy(ring[h], held.at[h], sems.at[h]) for h in range(rows)
    ]
    for copy in copies:
        copy.start()
    panel_ref[...] = front_ref[...]
    corner_ref[...] = jnp.zeros_like(corner_ref)
    for h in range(rows):
        for q in range(plan.lead_rows):
            block = rows * q + rem(row - h + rows, rows)

            @pl.when(block < NPIV)
            def _():
                corner_ref[block] = leads[h][q]

    across[...] = jnp.zeros_like(across)
    for copy in copies:
        copy.wait()

    def place(block):
        block_col, block_sub, slot = plan.dest(block)
        return (block_col ^ col) * plan.subs + (block_sub ^ sub), slot

    @pl.loop(0, plan.subs)
    def _(ms):
        @pl.loop(0, min(NPIV, plan.order))
        def _(j):
            pivot = maps_ref[ms, j]

            @pl.when(pivot < NPIV)
            def _():
                u = quot(j, plan.cols)
                m = (rem(j, plan.cols) ^ col) * plan.subs + ms

                @pl.loop(j, plan.order)
                def _(i):
                    block = maps_ref[ms, i]
                    h = rem(row - rem(i, rows) + rows, rows)
                    b = plan.offset(plan.first_start, quot(i, rows)) + u

                    @pl.when(rem(block, rows) == row)
                    def _():
                        panel_ref[quot(block, rows), pivot] += held[h, m, b]

                    @pl.when(block < NPIV)
                    def _():
                        corner_ref[block, pivot] += held[h, m, b]

                    @pl.when(rem(pivot, rows) == row)
                    def _():
                        target, slot = place(block)
                        across[target, quot(pivot, rows), slot] += held[h, m, b]

                    @pl.when((block < NPIV) & (block != pivot) & (rem(block, rows) == row))
                    def _():
                        target, slot = place(pivot)
                        across[target, quot(block, rows), slot] += held[h, m, b]

    for m in range(plan.plane):
        outs[m][...] = across[m]


def spread_kernel(plan, place_ref, maps_ref, *refs):
    rows = plan.rows
    ring_first = refs[:rows]
    ring_second = refs[rows : 2 * rows]
    outs = refs[2 * rows : 2 * rows + plan.plane]
    held, total, sems, out_sems = refs[2 * rows + plan.plane :]
    row, col, sub = place_ref[1], place_ref[2], place_ref[3]
    copies = []
    for h in range(rows):
        copies.append(
            pltpu.make_async_copy(
                ring_first[h], held.at[h, :, pl.ds(0, plan.first)], sems.at[h]
            )
        )
        copies.append(
            pltpu.make_async_copy(
                ring_second[h], held.at[h, :, pl.ds(plan.first, plan.second)], sems.at[rows + h]
            )
        )
    for copy in copies:
        copy.start()

    @pl.loop(0, plan.row_blocks)
    def _(t):
        for m in range(plan.plane):
            total[m, t] = jnp.zeros((plan.slots, plan.part, BLK), jnp.float32)

    for copy in copies:
        copy.wait()

    @pl.loop(0, plan.subs)
    def _(ms):
        @pl.loop(0, plan.order)
        def _(i):
            block_row = maps_ref[ms, i]

            @pl.when((rem(block_row, rows) == row) & (block_row >= NPIV))
            def _():
                @pl.loop(0, plan.order)
                def _(j):
                    block_col, block_sub, slot = plan.dest(maps_ref[ms, j])
                    high = jnp.maximum(i, j)
                    low = jnp.minimum(i, j)
                    h = rem(row - rem(high, rows) + rows, rows)
                    t = quot(high, rows)
                    u = quot(low, plan.cols)
                    m = (rem(low, plan.cols) ^ col) * plan.subs + ms
                    b = jnp.where(
                        u < plan.lead_cols,
                        plan.offset(plan.first_start, t) + u,
                        plan.first + plan.offset(plan.second_start, t) + u - plan.lead_cols,
                    )
                    target = (block_col ^ col) * plan.subs + (block_sub ^ sub)
                    total[target, quot(block_row, rows), slot] += held[h, m, b]

    out_copies = [
        pltpu.make_async_copy(total.at[m], outs[m], out_sems.at[m]) for m in range(plan.plane)
    ]
    for copy in out_copies:
        copy.start()
    for copy in out_copies:
        copy.wait()


def join_parts(plan, me, parts, block, column, scratch):
    for m, part in enumerate(parts):
        put_rows(scratch, 0, me ^ m, slice(None), part)
    joined = scratch[...]
    return jnp.where(column > block, joined.T, joined)


def lead_rows_kernel(plan, place_ref, front_ref, *refs):
    parts = refs[: plan.plane]
    out_ref, scratch = refs[plan.plane :]
    me, row, col, sub = place_ref[0], place_ref[1], place_ref[2], place_ref[3]
    for q in range(plan.lead_rows):
        block = plan.rows * q + row
        for slot in range(plan.slots):
            column = (sub * plan.slots + slot) * plan.cols + col
            joined = join_parts(
                plan, me, [part[q, slot] for part in parts], block, column, scratch
            )
            out_ref[q, :, slot * BLK : (slot + 1) * BLK] = (
                front_ref[q * BLK : (q + 1) * BLK, slot * BLK : (slot + 1) * BLK] + joined
            )


def corner_kernel(plan, place_ref, *refs):
    parts = refs[: plan.plane]
    out_ref = refs[plan.plane]
    me = place_ref[0]
    for m, part in enumerate(parts):
        for block in range(NPIV):
            for pivot in range(NPIV):
                put_rows(out_ref, block * BLK, me ^ m, block_lanes(pivot), part[block, pivot])


def halves(value):
    high = value.astype(jnp.bfloat16)
    return high, (value - high.astype(jnp.float32)).astype(jnp.bfloat16)


def right_kernel(plan, place_ref, inverse_ref, *refs):
    leads = refs[: plan.rows]
    high_ref, low_ref, stack = refs[plan.rows :]
    row = place_ref[1]
    for h in range(plan.rows):
        for q in range(plan.lead_rows):
            block = plan.rows * q + rem(row - h + plan.rows, plan.rows)

            @pl.when(block < NPIV)
            def _():
                stack[pl.ds(pl.multiple_of(block * BLK, BLK), BLK), :] = leads[h][q]

    for pivot in range(NPIV):
        depth = (pivot + 1) * BLK
        value = jnp.dot(
            inverse_ref[pivot * BLK : depth, :depth], stack[:depth, :],
            precision=highest, preferred_element_type=jnp.float32,
        )
        high, low = halves(value)
        high_ref[pivot * BLK : depth, :] = high
        low_ref[pivot * BLK : depth, :] = low


def left_kernel(plan, tile_blocks, half_steps, place_ref, inverse_ref, factor_ref, *refs):
    count = plan.plane
    first, second = refs[:count], refs[count : 2 * count]
    high_ref, low_ref, own_ref, panel, value_ref = refs[2 * count :]
    me, row, col = place_ref[0], place_ref[1], place_ref[2]
    step = pl.program_id(0)

    def load(parts):
        for t in range(tile_blocks):
            for m in range(count):
                for pivot in range(NPIV):
                    put_rows(panel, t * BLK, me ^ m, block_lanes(pivot), parts[m][t, pivot])

    @pl.when(step < half_steps)
    def _():
        load(first)

    @pl.when(step >= half_steps)
    def _():
        load(second)

    for pivot in range(NPIV):
        depth = (pivot + 1) * BLK
        value_ref[:, pivot * BLK : depth] = lax.dot_general(
            panel[:, :depth], inverse_ref[pivot * BLK : depth, :depth],
            (((1,), (1,)), ((), ())),
            precision=highest, preferred_element_type=jnp.float32,
        )
    high, low = halves(value_ref[...])
    high_ref[...] = high
    low_ref[...] = low
    for t in range(tile_blocks):
        block = plan.rows * (step * tile_blocks + t) + row
        for u in range(plan.lead_cols):
            pivot = jnp.minimum(plan.cols * u + col, NPIV - 1)
            lanes = pl.ds(pl.multiple_of(pivot * BLK, BLK), BLK)
            here = (slice(t * BLK, (t + 1) * BLK), slice(u * BLK, (u + 1) * BLK))
            own_ref[here] = value_ref[t * BLK : (t + 1) * BLK, lanes]

            @pl.when(block < NPIV)
            def _():
                own_ref[here] = factor_ref[
                    pl.ds(pl.multiple_of(block * BLK, BLK), BLK), lanes
                ]


def schur_kernel(plan, tile_blocks, place_ref, front_ref, high_ref, low_ref, own_ref,
                 right_high_ref, right_low_ref, *refs):
    parts = refs[: plan.plane]
    out_ref, scratch = refs[plan.plane :]
    me, row, col, sub = place_ref[0], place_ref[1], place_ref[2], place_ref[3]
    step = pl.program_id(0)
    update = jnp.dot(high_ref[...], right_high_ref[...], preferred_element_type=jnp.float32)
    update += jnp.dot(high_ref[...], right_low_ref[...], preferred_element_type=jnp.float32)
    update += jnp.dot(low_ref[...], right_high_ref[...], preferred_element_type=jnp.float32)
    out_ref[...] = front_ref[...] - update
    for t in range(tile_blocks):
        block = plan.rows * (step * tile_blocks + t) + row
        for slot in range(plan.slots):
            column = (sub * plan.slots + slot) * plan.cols + col
            here = (slice(t * BLK, (t + 1) * BLK), slice(slot * BLK, (slot + 1) * BLK))
            joined = join_parts(
                plan, me, [part[t, slot] for part in parts], block, column,
                scratch.at[t, slot],
            )
            value = out_ref[here] + joined
            value = jnp.where((block < NPIV) & (column >= NPIV), 0.0, value)
            if slot < plan.lead_cols:
                value = jnp.where(column < NPIV, own_ref[here], value)
            out_ref[here] = value


def swap(value, plan, bit):
    return lax.ppermute(value, PLANE, [(k, k ^ bit) for k in range(plan.plane)])


def gather_plane(value, plan, bits):
    held = {0: value}
    for bit in bits:
        for m in sorted(held):
            held[m ^ bit] = swap(held[m], plan, bit)
    return [held[m] for m in range(plan.plane)]


def ring_gather(value, plan):
    held = [value]
    for _ in range(1, plan.rows):
        held.append(
            lax.ppermute(held[-1], "row", [(r, (r + 1) % plan.rows) for r in range(plan.rows)])
        )
    return held


def body(front_entries, child_blocks, child_map):
    plan = Plan(front_entries.shape, child_blocks.shape)
    f32 = jnp.float32
    row = lax.axis_index("row").astype(jnp.int32)
    col = lax.axis_index("col").astype(jnp.int32)
    sub = lax.axis_index("sub").astype(jnp.int32)
    place = jnp.stack([col * plan.subs + sub, row, col, sub])
    vmem, smem, hbm = whole(pltpu.VMEM), whole(pltpu.SMEM), whole(pl.ANY)
    part, plane, rows = plan.part, plan.plane, plan.rows
    every = [(0, m) for m in range(1, plane)]

    maps = [child_map[0]]
    for m in range(1, plan.subs):
        maps.append(lax.ppermute(child_map[0], "sub", [(s, s ^ m) for s in range(plan.subs)]))
    maps = jnp.stack(maps)

    cut = pl.pallas_call(
        functools.partial(cut_child_kernel, plan),
        out_shape=[jax.ShapeDtypeStruct((plan.first + plan.second, part, BLK), f32)] * plane,
        in_specs=[smem, vmem],
        out_specs=[vmem] * plane,
        compiler_params=params(),
        name="cut_child",
    )(place, child_blocks)
    got = [cut[0]] + [swap(cut[m], plan, m) for m in range(1, plane)]
    ring_first = ring_gather(jnp.stack([g[: plan.first] for g in got]), plan)
    ring_second = ring_gather(jnp.stack([g[plan.first :] for g in got]), plan)

    lead_width = plan.lead_cols * BLK
    local_rows = front_entries.shape[0]
    front_cut = pl.pallas_call(
        functools.partial(cut_front_kernel, plan),
        grid=(1,),
        out_shape=[jax.ShapeDtypeStruct((plan.row_blocks, plan.lead_cols, part, BLK), f32)] * plane,
        in_specs=[smem, pl.BlockSpec((local_rows, lead_width), lambda g: (0, 0))],
        out_specs=[vmem] * plane,
        compiler_params=params(),
        name="cut_front",
    )(place, front_entries)
    owners = [k for k in range(plane) if k % plan.subs == 0]
    front_got = [front_cut[0]] + [
        lax.ppermute(front_cut[m], PLANE, [(k, k ^ m) for k in owners]) for m in range(1, plane)
    ]
    front_panel, front_lead = pl.pallas_call(
        functools.partial(front_panel_kernel, plan),
        out_shape=[
            jax.ShapeDtypeStruct((plan.row_blocks, NPIV, part, BLK), f32),
            jax.ShapeDtypeStruct((plan.lead_rows, NPIV, part, BLK), f32),
        ],
        in_specs=[smem] + [vmem] * plane,
        out_specs=[vmem] * 2,
        compiler_params=params(),
        name="front_panel",
    )(place, *front_got)
    leads = ring_gather(front_lead, plan)

    results = pl.pallas_call(
        functools.partial(panel_kernel, plan),
        out_shape=[
            jax.ShapeDtypeStruct((plan.row_blocks, NPIV, part, BLK), f32),
            jax.ShapeDtypeStruct((NPIV, NPIV, part, BLK), f32),
        ]
        + [jax.ShapeDtypeStruct((plan.lead_rows, plan.slots, part, BLK), f32)] * plane,
        in_specs=[smem, smem] + [hbm] * rows + [vmem] * (rows + 1),
        out_specs=[vmem] * (2 + plane),
        scratch_shapes=[
            pltpu.VMEM((rows, plane, plan.first, part, BLK), f32),
            pltpu.VMEM((plane, plan.lead_rows, plan.slots, part, BLK), f32),
            pltpu.SemaphoreType.DMA((rows,)),
        ],
        compiler_params=params(),
        name="panel",
    )(place, maps, *ring_first, *leads, front_panel)
    panel, corner_part, lead_parts = results[0], results[1], results[2:]

    bits = [1 << b for b in range(plane.bit_length() - 1)][::-1]
    other = bits[1:2] + bits[:1] + bits[2:]
    corner = pl.pallas_call(
        functools.partial(corner_kernel, plan),
        out_shape=jax.ShapeDtypeStruct((NPIV * BLK, NPIV * BLK), f32),
        in_specs=[smem] + [vmem] * plane,
        out_specs=vmem,
        compiler_params=params(),
        name="corner",
    )(place, *gather_plane(corner_part, plan, bits))
    factor = jnp.tril(lax.linalg.cholesky(corner, symmetrize_input=False))
    inverse = lax.linalg.triangular_solve(
        factor, jnp.eye(NPIV * BLK, dtype=f32), left_side=True, lower=True
    )

    lead_got = [lead_parts[0]] + [swap(lead_parts[m], plan, m) for m in range(1, plane)]
    lead_rows = pl.pallas_call(
        functools.partial(lead_rows_kernel, plan),
        grid=(1,),
        out_shape=jax.ShapeDtypeStruct((plan.lead_rows, BLK, plan.slots * BLK), f32),
        in_specs=[smem, pl.BlockSpec((plan.lead_rows * BLK, plan.slots * BLK), lambda g: (0, 0))]
        + [vmem] * plane,
        out_specs=vmem,
        scratch_shapes=[pltpu.VMEM((BLK, BLK), f32)],
        compiler_params=params(),
        name="lead_rows",
    )(place, front_entries, *lead_got)
    lead_ring = ring_gather(lead_rows, plan)
    right_high, right_low = pl.pallas_call(
        functools.partial(right_kernel, plan),
        out_shape=[jax.ShapeDtypeStruct((NPIV * BLK, plan.slots * BLK), jnp.bfloat16)] * 2,
        in_specs=[smem, vmem] + [vmem] * rows,
        out_specs=[vmem] * 2,
        scratch_shapes=[pltpu.VMEM((NPIV * BLK, plan.slots * BLK), f32)],
        compiler_params=params(),
        name="right_factor",
    )(place, inverse, *lead_ring)

    half = plan.row_blocks // 2
    panel_first = gather_plane(panel[:half], plan, bits)
    panel_second = gather_plane(panel[half:], plan, other)
    tile = 2
    half_steps = half // tile
    left_high, left_low, own = pl.pallas_call(
        functools.partial(left_kernel, plan, tile, half_steps),
        grid=(2 * half_steps,),
        out_shape=[
            jax.ShapeDtypeStruct((local_rows, NPIV * BLK), jnp.bfloat16),
            jax.ShapeDtypeStruct((local_rows, NPIV * BLK), jnp.bfloat16),
            jax.ShapeDtypeStruct((local_rows, lead_width), f32),
        ],
        in_specs=[smem, vmem, vmem]
        + [
            pl.BlockSpec(
                (tile, NPIV, part, BLK), lambda g: (jnp.minimum(g, half_steps - 1), 0, 0, 0)
            )
        ]
        * plane
        + [
            pl.BlockSpec(
                (tile, NPIV, part, BLK), lambda g: (jnp.maximum(g - half_steps, 0), 0, 0, 0)
            )
        ]
        * plane,
        out_specs=[
            pl.BlockSpec((tile * BLK, NPIV * BLK), lambda g: (g, 0)),
            pl.BlockSpec((tile * BLK, NPIV * BLK), lambda g: (g, 0)),
            pl.BlockSpec((tile * BLK, lead_width), lambda g: (g, 0)),
        ],
        scratch_shapes=[
            pltpu.VMEM((tile * BLK, NPIV * BLK), f32),
            pltpu.VMEM((tile * BLK, NPIV * BLK), f32),
        ],
        compiler_params=params(),
        name="left_factor",
    )(place, inverse, factor, *panel_first, *panel_second)

    spread = pl.pallas_call(
        functools.partial(spread_kernel, plan),
        out_shape=[jax.ShapeDtypeStruct((plan.row_blocks, plan.slots, part, BLK), f32)] * plane,
        in_specs=[smem, smem] + [hbm] * (2 * rows),
        out_specs=[hbm] * plane,
        scratch_shapes=[
            pltpu.VMEM((rows, plane, plan.first + plan.second, part, BLK), f32),
            pltpu.VMEM((plane, plan.row_blocks, plan.slots, part, BLK), f32),
            pltpu.SemaphoreType.DMA((2 * rows,)),
            pltpu.SemaphoreType.DMA((plane,)),
        ],
        compiler_params=params(),
        name="spread",
    )(place, maps, *ring_first, *ring_second)
    spread_got = [spread[0]] + [swap(spread[m], plan, m) for m in range(1, plane)]

    full = lambda g: (0, 0)
    by_row = lambda g: (g, 0)
    width = plan.slots * BLK
    return pl.pallas_call(
        functools.partial(schur_kernel, plan, tile),
        grid=(plan.row_blocks // tile,),
        out_shape=jax.ShapeDtypeStruct(front_entries.shape, f32),
        in_specs=[
            smem,
            pl.BlockSpec((tile * BLK, width), by_row),
            pl.BlockSpec((tile * BLK, NPIV * BLK), by_row),
            pl.BlockSpec((tile * BLK, NPIV * BLK), by_row),
            pl.BlockSpec((tile * BLK, lead_width), by_row),
            pl.BlockSpec((NPIV * BLK, width), full),
            pl.BlockSpec((NPIV * BLK, width), full),
        ]
        + [pl.BlockSpec((tile, plan.slots, part, BLK), lambda g: (g, 0, 0, 0))] * plane,
        out_specs=pl.BlockSpec((tile * BLK, width), by_row),
        scratch_shapes=[pltpu.VMEM((tile, plan.slots, BLK, BLK), f32)],
        compiler_params=params(),
        name="schur",
    )(place, front_entries, left_high, left_low, own, right_high, right_low, *spread_got)


def solution(mesh):
    placed = (P("row", ("col", "sub")), P("sub", "row", "col"), P("sub", None))
    return jax.shard_map(
        body, mesh=mesh, in_specs=placed, out_specs=P("row", ("col", "sub")), check_vma=False
    )
```

```python
import functools

import jax
import jax.numpy as jnp
from jax import lax
from jax.experimental import pallas as pl
from jax.experimental.pallas import tpu as pltpu
from jax.sharding import PartitionSpec as P

BLK = 128
NPIV = 6
PLANE = ("col", "sub")
VMEM_BYTES = 60 * 1024 * 1024

highest = lax.Precision.HIGHEST


def quot(value, number):
    if number & (number - 1) == 0:
        return lax.shift_right_logical(value, jnp.int32(number.bit_length() - 1))
    return lax.div(value, jnp.int32(number))


def rem(value, number):
    if number & (number - 1) == 0:
        return value & (number - 1)
    return lax.rem(value, jnp.int32(number))


def whole(memory):
    return pl.BlockSpec(memory_space=memory)


def params(**more):
    return pltpu.CompilerParams(vmem_limit_bytes=VMEM_BYTES, **more)


class Plan:
    def __init__(self, front_shape, child_shape):
        self.rows = lax.axis_size("row")
        self.cols = lax.axis_size("col")
        self.subs = lax.axis_size("sub")
        self.plane = self.cols * self.subs
        self.part = BLK // self.plane
        self.row_blocks = front_shape[0] // BLK
        self.slots = front_shape[1] // BLK
        self.child_rows = child_shape[1] // BLK
        self.child_cols = child_shape[2] // BLK
        self.order = self.child_rows * self.rows
        self.lead_cols = -(-NPIV // self.cols)
        self.lead_rows = -(-NPIV // self.rows)
        reach = [
            min((self.rows * t + self.rows - 1) // self.cols + 1, self.child_cols)
            for t in range(self.child_rows)
        ]
        first = [(t, u) for t in range(self.child_rows) for u in range(min(reach[t], self.lead_cols))]
        second = [(t, u) for t in range(self.child_rows) for u in range(self.lead_cols, reach[t])]
        self.first = len(first)
        self.second = len(second)
        self.blocks = first + second
        self.first_start = [first.index((t, 0)) for t in range(self.child_rows)]
        self.second_start = [
            sum(1 for b in second if b[0] < t) for t in range(self.child_rows)
        ]

    def dest(self, block):
        high = quot(block, self.cols)
        return rem(block, self.cols), quot(high, self.slots), rem(high, self.slots)

    def offset(self, starts, t):
        out = jnp.int32(starts[0])
        for step in range(1, len(starts)):
            out = jnp.where(t == step, jnp.int32(starts[step]), out)
        return out


def take_rows(ref, lead, base, index, part, lanes):
    if part % 8 == 0:
        return ref[(*lead, pl.ds(pl.multiple_of(base + index * part, part), part), lanes)]
    share = 8 // part
    group = ref[(*lead, pl.ds(pl.multiple_of(base + quot(index, share) * 8, 8), 8), lanes)]
    out = group[:part]
    for step in range(1, share):
        out = jnp.where(rem(index, share) == step, group[step * part : (step + 1) * part], out)
    return out


def put_rows(ref, base, index, lanes, value):
    part = value.shape[0]
    if part % 8 == 0:
        ref[pl.ds(pl.multiple_of(base + index * part, part), part), lanes] = value
        return
    share = 8 // part
    rows = pl.ds(pl.multiple_of(base + quot(index, share) * 8, 8), 8)
    spot = lax.broadcasted_iota(jnp.int32, (8, value.shape[1]), 0)
    mine = quot(spot, part) == rem(index, share)
    ref[rows, lanes] = jnp.where(mine, jnp.concatenate([value] * share, axis=0), ref[rows, lanes])


def block_lanes(number):
    return slice(number * BLK, (number + 1) * BLK)


def cut_child_kernel(plan, place_ref, tile_ref, *out_refs):
    me = place_ref[0]
    for m, out_ref in enumerate(out_refs):
        for b, (t, u) in enumerate(plan.blocks):
            out_ref[b] = take_rows(tile_ref, (0,), t * BLK, me ^ m, plan.part, block_lanes(u))


def cut_front_kernel(plan, place_ref, front_ref, *out_refs):
    me = place_ref[0]

    @pl.loop(0, plan.row_blocks)
    def _(t):
        for m, out_ref in enumerate(out_refs):
            for u in range(plan.lead_cols):
                out_ref[t, u] = take_rows(front_ref, (), t * BLK, me ^ m, plan.part, block_lanes(u))


def front_panel_kernel(plan, place_ref, *refs):
    pieces = refs[: plan.plane]
    panel_ref, lead_ref = refs[plan.plane :]
    col, sub = place_ref[2], place_ref[3]
    panel_ref[...] = jnp.zeros_like(panel_ref)
    for mc in range(plan.cols):
        for u in range(plan.lead_cols):
            pivot = plan.cols * u + (col ^ mc)

            @pl.when(pivot < NPIV)
            def _():
                @pl.loop(0, plan.row_blocks)
                def _(t):
                    total = jnp.zeros((plan.part, BLK), jnp.float32)
                    for ms in range(plan.subs):
                        piece = pieces[mc * plan.subs + ms][t, u]
                        if mc == 0 and ms == 0:
                            piece = jnp.where(sub == 0, piece, 0.0)
                        total = total + piece
                    panel_ref[t, pivot] = total

    lead_ref[...] = panel_ref[: plan.lead_rows]


def panel_kernel(plan, place_ref, maps_ref, *refs):
    rows = plan.rows
    ring = refs[:rows]
    leads = refs[rows : 2 * rows]
    front_ref = refs[2 * rows]
    panel_ref, corner_ref = refs[2 * rows + 1 : 2 * rows + 3]
    outs = refs[2 * rows + 3 : 2 * rows + 3 + plan.plane]
    held, across, sems = refs[2 * rows + 3 + plan.plane :]
    row, col, sub = place_ref[1], place_ref[2], place_ref[3]
    copies = [
        pltpu.make_async_copy(ring[h], held.at[h], sems.at[h]) for h in range(rows)
    ]
    for copy in copies:
        copy.start()
    panel_ref[...] = front_ref[...]
    corner_ref[...] = jnp.zeros_like(corner_ref)
    for h in range(rows):
        for q in range(plan.lead_rows):
            block = rows * q + rem(row - h + rows, rows)

            @pl.when(block < NPIV)
            def _():
                corner_ref[block] = leads[h][q]

    across[...] = jnp.zeros_like(across)
    for copy in copies:
        copy.wait()

    def place(block):
        block_col, block_sub, slot = plan.dest(block)
        return (block_col ^ col) * plan.subs + (block_sub ^ sub), slot

    @pl.loop(0, plan.subs)
    def _(ms):
        @pl.loop(0, min(NPIV, plan.order))
        def _(j):
            pivot = maps_ref[ms, j]

            @pl.when(pivot < NPIV)
            def _():
                u = quot(j, plan.cols)
                m = (rem(j, plan.cols) ^ col) * plan.subs + ms

                @pl.loop(j, plan.order)
                def _(i):
                    block = maps_ref[ms, i]
                    h = rem(row - rem(i, rows) + rows, rows)
                    b = plan.offset(plan.first_start, quot(i, rows)) + u

                    @pl.when(rem(block, rows) == row)
                    def _():
                        panel_ref[quot(block, rows), pivot] += held[h, m, b]

                    @pl.when(block < NPIV)
                    def _():
                        corner_ref[block, pivot] += held[h, m, b]

                    @pl.when(rem(pivot, rows) == row)
                    def _():
                        target, slot = place(block)
                        across[target, quot(pivot, rows), slot] += held[h, m, b]

                    @pl.when((block < NPIV) & (block != pivot) & (rem(block, rows) == row))
                    def _():
                        target, slot = place(pivot)
                        across[target, quot(block, rows), slot] += held[h, m, b]

    for m in range(plan.plane):
        outs[m][...] = across[m]


def spread_kernel(plan, place_ref, maps_ref, *refs):
    rows = plan.rows
    ring_first = refs[:rows]
    ring_second = refs[rows : 2 * rows]
    outs = refs[2 * rows : 2 * rows + plan.plane]
    held, total, sems, out_sems = refs[2 * rows + plan.plane :]
    row, col, sub = place_ref[1], place_ref[2], place_ref[3]
    copies = []
    for h in range(rows):
        copies.append(
            pltpu.make_async_copy(
                ring_first[h], held.at[h, :, pl.ds(0, plan.first)], sems.at[h]
            )
        )
        copies.append(
            pltpu.make_async_copy(
                ring_second[h], held.at[h, :, pl.ds(plan.first, plan.second)], sems.at[rows + h]
            )
        )
    for copy in copies:
        copy.start()

    @pl.loop(0, plan.row_blocks)
    def _(t):
        for m in range(plan.plane):
            total[m, t] = jnp.zeros((plan.slots, plan.part, BLK), jnp.float32)

    for copy in copies:
        copy.wait()

    @pl.loop(0, plan.subs)
    def _(ms):
        @pl.loop(0, plan.order)
        def _(i):
            block_row = maps_ref[ms, i]

            @pl.when((rem(block_row, rows) == row) & (block_row >= NPIV))
            def _():
                @pl.loop(0, plan.order)
                def _(j):
                    block_col, block_sub, slot = plan.dest(maps_ref[ms, j])
                    high = jnp.maximum(i, j)
                    low = jnp.minimum(i, j)
                    h = rem(row - rem(high, rows) + rows, rows)
                    t = quot(high, rows)
                    u = quot(low, plan.cols)
                    m = (rem(low, plan.cols) ^ col) * plan.subs + ms
                    b = jnp.where(
                        u < plan.lead_cols,
                        plan.offset(plan.first_start, t) + u,
                        plan.first + plan.offset(plan.second_start, t) + u - plan.lead_cols,
                    )
                    target = (block_col ^ col) * plan.subs + (block_sub ^ sub)
                    total[target, quot(block_row, rows), slot] += held[h, m, b]

    out_copies = [
        pltpu.make_async_copy(total.at[m], outs[m], out_sems.at[m]) for m in range(plan.plane)
    ]
    for copy in out_copies:
        copy.start()
    for copy in out_copies:
        copy.wait()


def join_parts(plan, me, parts, block, column, scratch):
    for m, part in enumerate(parts):
        put_rows(scratch, 0, me ^ m, slice(None), part)
    joined = scratch[...]
    return jnp.where(column > block, joined.T, joined)


def lead_rows_kernel(plan, place_ref, front_ref, *refs):
    parts = refs[: plan.plane]
    out_ref, scratch = refs[plan.plane :]
    me, row, col, sub = place_ref[0], place_ref[1], place_ref[2], place_ref[3]
    for q in range(plan.lead_rows):
        block = plan.rows * q + row
        for slot in range(plan.slots):
            column = (sub * plan.slots + slot) * plan.cols + col
            joined = join_parts(
                plan, me, [part[q, slot] for part in parts], block, column, scratch
            )
            out_ref[q, :, slot * BLK : (slot + 1) * BLK] = (
                front_ref[q * BLK : (q + 1) * BLK, slot * BLK : (slot + 1) * BLK] + joined
            )


def spread_lane(value, lane):
    return jnp.broadcast_to(value[:, lane : lane + 1], value.shape)


def spread_row(value, row):
    return jnp.broadcast_to(value[row : row + 1, :], value.shape)


def factor_block(matrix):
    group = 8
    count = BLK // group
    shape = (group, BLK)
    at_row = lax.broadcasted_iota(jnp.int32, shape, 0)
    at_lane = lax.broadcasted_iota(jnp.int32, shape, 1)
    left = [matrix[group * s : group * (s + 1), :] for s in range(count)]
    right = [jnp.where(at_lane == at_row + group * s, 1.0, 0.0) for s in range(count)]
    for s in range(count):
        cols = {
            t: [spread_lane(left[t], group * s + q) for q in range(group)] for t in range(s, count)
        }
        for o in range(group):
            inverse = 1.0 / spread_row(cols[s][o], o)
            scale = [spread_row(cols[s][q], o) * inverse for q in range(o + 1, group)]
            row_left = spread_row(left[s], o) * inverse
            row_right = spread_row(right[s], o) * inverse
            for t in range(s, count):
                col = cols[t][o]
                if t == s:
                    col = jnp.where(at_row > o, col, 0.0)
                for q in range(o + 1, group):
                    cols[t][q] = cols[t][q] - col * scale[q - o - 1]
                left[t] = left[t] - col * row_left
                right[t] = right[t] - col * row_right
    for s in range(count):
        pivots = jnp.sum(
            jnp.where(at_lane == at_row + group * s, left[s], 0.0), axis=1, keepdims=True
        )
        root = lax.rsqrt(pivots)
        root = root * (1.5 - 0.5 * pivots * root * root)
        left[s] = jnp.where(at_lane >= at_row + group * s, left[s] * root, 0.0)
        right[s] = right[s] * root
    return jnp.concatenate(left, axis=0), jnp.concatenate(right, axis=0)


def corner_kernel(plan, place_ref, *refs):
    parts = refs[: plan.plane]
    factor_ref, work = refs[plan.plane :]
    me = place_ref[0]
    for m, part in enumerate(parts):
        for block in range(NPIV):
            for pivot in range(block + 1):
                put_rows(work, block * BLK, me ^ m, block_lanes(pivot), part[block, pivot])
    for block in range(NPIV):
        for pivot in range(block):
            work[block_lanes(pivot), block_lanes(block)] = work[
                block_lanes(block), block_lanes(pivot)
            ].T

    exact = functools.partial(
        lax.dot_general, precision=highest, preferred_element_type=jnp.float32
    )
    factor_ref[...] = jnp.zeros_like(factor_ref)

    @pl.loop(0, NPIV)
    def _(pivot):
        here = pl.ds(pl.multiple_of(pivot * BLK, BLK), BLK)
        upper, inverse = factor_block(work[here, here])
        factor_ref[here, here] = upper.T
        work[here, :] = exact(inverse, work[here, :], (((1,), (0,)), ((), ())))
        work[here, here] = inverse

        @pl.loop(pivot + 1, NPIV)
        def _(block):
            there = pl.ds(pl.multiple_of(block * BLK, BLK), BLK)
            lower = work[here, there].T
            factor_ref[there, here] = lower
            work[there, here] = jnp.zeros((BLK, BLK), jnp.float32)
            work[there, :] -= exact(lower, work[here, :], (((1,), (0,)), ((), ())))


def halves(value):
    high = value.astype(jnp.bfloat16)
    return high, (value - high.astype(jnp.float32)).astype(jnp.bfloat16)


def right_kernel(plan, place_ref, inverse_ref, *refs):
    leads = refs[: plan.rows]
    high_ref, low_ref, stack = refs[plan.rows :]
    row = place_ref[1]
    for h in range(plan.rows):
        for q in range(plan.lead_rows):
            block = plan.rows * q + rem(row - h + plan.rows, plan.rows)

            @pl.when(block < NPIV)
            def _():
                stack[pl.ds(pl.multiple_of(block * BLK, BLK), BLK), :] = leads[h][q]

    for pivot in range(NPIV):
        depth = (pivot + 1) * BLK
        value = jnp.dot(
            inverse_ref[pivot * BLK : depth, :depth], stack[:depth, :],
            precision=highest, preferred_element_type=jnp.float32,
        )
        high, low = halves(value)
        high_ref[pivot * BLK : depth, :] = high
        low_ref[pivot * BLK : depth, :] = low


def left_kernel(plan, tile_blocks, half_steps, place_ref, inverse_ref, factor_ref, *refs):
    count = plan.plane
    first, second = refs[:count], refs[count : 2 * count]
    high_ref, low_ref, own_ref, panel, value_ref = refs[2 * count :]
    me, row, col = place_ref[0], place_ref[1], place_ref[2]
    step = pl.program_id(0)

    def load(parts):
        for t in range(tile_blocks):
            for m in range(count):
                for pivot in range(NPIV):
                    put_rows(panel, t * BLK, me ^ m, block_lanes(pivot), parts[m][t, pivot])

    @pl.when(step < half_steps)
    def _():
        load(first)

    @pl.when(step >= half_steps)
    def _():
        load(second)

    for pivot in range(NPIV):
        depth = (pivot + 1) * BLK
        value_ref[:, pivot * BLK : depth] = lax.dot_general(
            panel[:, :depth], inverse_ref[pivot * BLK : depth, :depth],
            (((1,), (1,)), ((), ())),
            precision=highest, preferred_element_type=jnp.float32,
        )
    high, low = halves(value_ref[...])
    high_ref[...] = high
    low_ref[...] = low
    for t in range(tile_blocks):
        block = plan.rows * (step * tile_blocks + t) + row
        for u in range(plan.lead_cols):
            pivot = jnp.minimum(plan.cols * u + col, NPIV - 1)
            lanes = pl.ds(pl.multiple_of(pivot * BLK, BLK), BLK)
            here = (slice(t * BLK, (t + 1) * BLK), slice(u * BLK, (u + 1) * BLK))
            own_ref[here] = value_ref[t * BLK : (t + 1) * BLK, lanes]

            @pl.when(block < NPIV)
            def _():
                own_ref[here] = factor_ref[
                    pl.ds(pl.multiple_of(block * BLK, BLK), BLK), lanes
                ]


def schur_kernel(plan, tile_blocks, place_ref, front_ref, high_ref, low_ref, own_ref,
                 right_high_ref, right_low_ref, *refs):
    parts = refs[: plan.plane]
    out_ref, scratch = refs[plan.plane :]
    me, row, col, sub = place_ref[0], place_ref[1], place_ref[2], place_ref[3]
    step = pl.program_id(0)
    update = jnp.dot(high_ref[...], right_high_ref[...], preferred_element_type=jnp.float32)
    update += jnp.dot(high_ref[...], right_low_ref[...], preferred_element_type=jnp.float32)
    update += jnp.dot(low_ref[...], right_high_ref[...], preferred_element_type=jnp.float32)
    out_ref[...] = front_ref[...] - update
    for t in range(tile_blocks):
        block = plan.rows * (step * tile_blocks + t) + row
        for slot in range(plan.slots):
            column = (sub * plan.slots + slot) * plan.cols + col
            here = (slice(t * BLK, (t + 1) * BLK), slice(slot * BLK, (slot + 1) * BLK))
            joined = join_parts(
                plan, me, [part[t, slot] for part in parts], block, column,
                scratch.at[t, slot],
            )
            value = out_ref[here] + joined
            value = jnp.where((block < NPIV) & (column >= NPIV), 0.0, value)
            if slot < plan.lead_cols:
                value = jnp.where(column < NPIV, own_ref[here], value)
            out_ref[here] = value


def swap(value, plan, bit):
    return lax.ppermute(value, PLANE, [(k, k ^ bit) for k in range(plan.plane)])


def gather_plane(value, plan, bits):
    held = {0: value}
    for bit in bits:
        for m in sorted(held):
            held[m ^ bit] = swap(held[m], plan, bit)
    return [held[m] for m in range(plan.plane)]


def ring_gather(value, plan):
    held = [value]
    for _ in range(1, plan.rows):
        held.append(
            lax.ppermute(held[-1], "row", [(r, (r + 1) % plan.rows) for r in range(plan.rows)])
        )
    return held


def body(front_entries, child_blocks, child_map):
    plan = Plan(front_entries.shape, child_blocks.shape)
    f32 = jnp.float32
    row = lax.axis_index("row").astype(jnp.int32)
    col = lax.axis_index("col").astype(jnp.int32)
    sub = lax.axis_index("sub").astype(jnp.int32)
    place = jnp.stack([col * plan.subs + sub, row, col, sub])
    vmem, smem, hbm = whole(pltpu.VMEM), whole(pltpu.SMEM), whole(pl.ANY)
    part, plane, rows = plan.part, plan.plane, plan.rows
    every = [(0, m) for m in range(1, plane)]

    maps = [child_map[0]]
    for m in range(1, plan.subs):
        maps.append(lax.ppermute(child_map[0], "sub", [(s, s ^ m) for s in range(plan.subs)]))
    maps = jnp.stack(maps)

    cut = pl.pallas_call(
        functools.partial(cut_child_kernel, plan),
        out_shape=[jax.ShapeDtypeStruct((plan.first + plan.second, part, BLK), f32)] * plane,
        in_specs=[smem, vmem],
        out_specs=[vmem] * plane,
        compiler_params=params(),
        name="cut_child",
    )(place, child_blocks)
    got = [cut[0]] + [swap(cut[m], plan, m) for m in range(1, plane)]
    ring_first = ring_gather(jnp.stack([g[: plan.first] for g in got]), plan)
    ring_second = ring_gather(jnp.stack([g[plan.first :] for g in got]), plan)

    lead_width = plan.lead_cols * BLK
    local_rows = front_entries.shape[0]
    front_cut = pl.pallas_call(
        functools.partial(cut_front_kernel, plan),
        grid=(1,),
        out_shape=[jax.ShapeDtypeStruct((plan.row_blocks, plan.lead_cols, part, BLK), f32)] * plane,
        in_specs=[smem, pl.BlockSpec((local_rows, lead_width), lambda g: (0, 0))],
        out_specs=[vmem] * plane,
        compiler_params=params(),
        name="cut_front",
    )(place, front_entries)
    owners = [k for k in range(plane) if k % plan.subs == 0]
    front_got = [front_cut[0]] + [
        lax.ppermute(front_cut[m], PLANE, [(k, k ^ m) for k in owners]) for m in range(1, plane)
    ]
    front_panel, front_lead = pl.pallas_call(
        functools.partial(front_panel_kernel, plan),
        out_shape=[
            jax.ShapeDtypeStruct((plan.row_blocks, NPIV, part, BLK), f32),
            jax.ShapeDtypeStruct((plan.lead_rows, NPIV, part, BLK), f32),
        ],
        in_specs=[smem] + [vmem] * plane,
        out_specs=[vmem] * 2,
        compiler_params=params(),
        name="front_panel",
    )(place, *front_got)
    leads = ring_gather(front_lead, plan)

    results = pl.pallas_call(
        functools.partial(panel_kernel, plan),
        out_shape=[
            jax.ShapeDtypeStruct((plan.row_blocks, NPIV, part, BLK), f32),
            jax.ShapeDtypeStruct((NPIV, NPIV, part, BLK), f32),
        ]
        + [jax.ShapeDtypeStruct((plan.lead_rows, plan.slots, part, BLK), f32)] * plane,
        in_specs=[smem, smem] + [hbm] * rows + [vmem] * (rows + 1),
        out_specs=[vmem] * (2 + plane),
        scratch_shapes=[
            pltpu.VMEM((rows, plane, plan.first, part, BLK), f32),
            pltpu.VMEM((plane, plan.lead_rows, plan.slots, part, BLK), f32),
            pltpu.SemaphoreType.DMA((rows,)),
        ],
        compiler_params=params(),
        name="panel",
    )(place, maps, *ring_first, *leads, front_panel)
    panel, corner_part, lead_parts = results[0], results[1], results[2:]

    bits = [1 << b for b in range(plane.bit_length() - 1)][::-1]
    other = bits[1:2] + bits[:1] + bits[2:]
    factor, inverse = pl.pallas_call(
        functools.partial(corner_kernel, plan),
        out_shape=[jax.ShapeDtypeStruct((NPIV * BLK, NPIV * BLK), f32)] * 2,
        in_specs=[smem] + [vmem] * plane,
        out_specs=[vmem] * 2,
        compiler_params=params(),
        name="corner",
    )(place, *gather_plane(corner_part, plan, bits))

    lead_got = [lead_parts[0]] + [swap(lead_parts[m], plan, m) for m in range(1, plane)]
    lead_rows = pl.pallas_call(
        functools.partial(lead_rows_kernel, plan),
        grid=(1,),
        out_shape=jax.ShapeDtypeStruct((plan.lead_rows, BLK, plan.slots * BLK), f32),
        in_specs=[smem, pl.BlockSpec((plan.lead_rows * BLK, plan.slots * BLK), lambda g: (0, 0))]
        + [vmem] * plane,
        out_specs=vmem,
        scratch_shapes=[pltpu.VMEM((BLK, BLK), f32)],
        compiler_params=params(),
        name="lead_rows",
    )(place, front_entries, *lead_got)
    lead_ring = ring_gather(lead_rows, plan)
    right_high, right_low = pl.pallas_call(
        functools.partial(right_kernel, plan),
        out_shape=[jax.ShapeDtypeStruct((NPIV * BLK, plan.slots * BLK), jnp.bfloat16)] * 2,
        in_specs=[smem, vmem] + [vmem] * rows,
        out_specs=[vmem] * 2,
        scratch_shapes=[pltpu.VMEM((NPIV * BLK, plan.slots * BLK), f32)],
        compiler_params=params(),
        name="right_factor",
    )(place, inverse, *lead_ring)

    half = plan.row_blocks // 2
    panel_first = gather_plane(panel[:half], plan, bits)
    panel_second = gather_plane(panel[half:], plan, other)
    tile = 2
    half_steps = half // tile
    left_high, left_low, own = pl.pallas_call(
        functools.partial(left_kernel, plan, tile, half_steps),
        grid=(2 * half_steps,),
        out_shape=[
            jax.ShapeDtypeStruct((local_rows, NPIV * BLK), jnp.bfloat16),
            jax.ShapeDtypeStruct((local_rows, NPIV * BLK), jnp.bfloat16),
            jax.ShapeDtypeStruct((local_rows, lead_width), f32),
        ],
        in_specs=[smem, vmem, vmem]
        + [
            pl.BlockSpec(
                (tile, NPIV, part, BLK), lambda g: (jnp.minimum(g, half_steps - 1), 0, 0, 0)
            )
        ]
        * plane
        + [
            pl.BlockSpec(
                (tile, NPIV, part, BLK), lambda g: (jnp.maximum(g - half_steps, 0), 0, 0, 0)
            )
        ]
        * plane,
        out_specs=[
            pl.BlockSpec((tile * BLK, NPIV * BLK), lambda g: (g, 0)),
            pl.BlockSpec((tile * BLK, NPIV * BLK), lambda g: (g, 0)),
            pl.BlockSpec((tile * BLK, lead_width), lambda g: (g, 0)),
        ],
        scratch_shapes=[
            pltpu.VMEM((tile * BLK, NPIV * BLK), f32),
            pltpu.VMEM((tile * BLK, NPIV * BLK), f32),
        ],
        compiler_params=params(),
        name="left_factor",
    )(place, inverse, factor, *panel_first, *panel_second)

    spread = pl.pallas_call(
        functools.partial(spread_kernel, plan),
        out_shape=[jax.ShapeDtypeStruct((plan.row_blocks, plan.slots, part, BLK), f32)] * plane,
        in_specs=[smem, smem] + [hbm] * (2 * rows),
        out_specs=[hbm] * plane,
        scratch_shapes=[
            pltpu.VMEM((rows, plane, plan.first + plan.second, part, BLK), f32),
            pltpu.VMEM((plane, plan.row_blocks, plan.slots, part, BLK), f32),
            pltpu.SemaphoreType.DMA((2 * rows,)),
            pltpu.SemaphoreType.DMA((plane,)),
        ],
        compiler_params=params(),
        name="spread",
    )(place, maps, *ring_first, *ring_second)
    spread_got = [spread[0]] + [swap(spread[m], plan, m) for m in range(1, plane)]

    full = lambda g: (0, 0)
    by_row = lambda g: (g, 0)
    width = plan.slots * BLK
    return pl.pallas_call(
        functools.partial(schur_kernel, plan, tile),
        grid=(plan.row_blocks // tile,),
        out_shape=jax.ShapeDtypeStruct(front_entries.shape, f32),
        in_specs=[
            smem,
            pl.BlockSpec((tile * BLK, width), by_row),
            pl.BlockSpec((tile * BLK, NPIV * BLK), by_row),
            pl.BlockSpec((tile * BLK, NPIV * BLK), by_row),
            pl.BlockSpec((tile * BLK, lead_width), by_row),
            pl.BlockSpec((NPIV * BLK, width), full),
            pl.BlockSpec((NPIV * BLK, width), full),
        ]
        + [pl.BlockSpec((tile, plan.slots, part, BLK), lambda g: (g, 0, 0, 0))] * plane,
        out_specs=pl.BlockSpec((tile * BLK, width), by_row),
        scratch_shapes=[pltpu.VMEM((tile, plan.slots, BLK, BLK), f32)],
        compiler_params=params(),
        name="schur",
    )(place, front_entries, left_high, left_low, own, right_high, right_low, *spread_got)


def solution(mesh):
    placed = (P("row", ("col", "sub")), P("sub", "row", "col"), P("sub", None))
    return jax.shard_map(
        body, mesh=mesh, in_specs=placed, out_specs=P("row", ("col", "sub")), check_vma=False
    )
```

```python
import functools

import jax
import jax.numpy as jnp
from jax import lax
from jax.experimental import pallas as pl
from jax.experimental.pallas import tpu as pltpu
from jax.sharding import PartitionSpec as P

BLK = 128
NPIV = 6
PLANE = ("col", "sub")
VMEM_BYTES = 60 * 1024 * 1024

highest = lax.Precision.HIGHEST


def quot(value, number):
    if number & (number - 1) == 0:
        return lax.shift_right_logical(value, jnp.int32(number.bit_length() - 1))
    return lax.div(value, jnp.int32(number))


def rem(value, number):
    if number & (number - 1) == 0:
        return value & (number - 1)
    return lax.rem(value, jnp.int32(number))


def whole(memory):
    return pl.BlockSpec(memory_space=memory)


def cost(micros):
    return pl.CostEstimate(
        flops=micros * 1_000_000_000, bytes_accessed=micros * 3_000_000, transcendentals=0
    )


def params(**more):
    return pltpu.CompilerParams(vmem_limit_bytes=VMEM_BYTES, **more)


class Plan:
    def __init__(self, front_shape, child_shape):
        self.rows = lax.axis_size("row")
        self.cols = lax.axis_size("col")
        self.subs = lax.axis_size("sub")
        self.plane = self.cols * self.subs
        self.part = BLK // self.plane
        self.row_blocks = front_shape[0] // BLK
        self.slots = front_shape[1] // BLK
        self.child_rows = child_shape[1] // BLK
        self.child_cols = child_shape[2] // BLK
        self.order = self.child_rows * self.rows
        self.lead_cols = -(-NPIV // self.cols)
        self.lead_rows = -(-NPIV // self.rows)
        reach = [
            min((self.rows * t + self.rows - 1) // self.cols + 1, self.child_cols)
            for t in range(self.child_rows)
        ]
        first = [(t, u) for t in range(self.child_rows) for u in range(min(reach[t], self.lead_cols))]
        second = [(t, u) for t in range(self.child_rows) for u in range(self.lead_cols, reach[t])]
        self.first = len(first)
        self.second = len(second)
        self.blocks = first + second
        self.rest = self.second + self.row_blocks * self.lead_cols + 1
        self.area = self.row_blocks * self.slots
        self.limit = self.area // 2
        self.first_start = [first.index((t, 0)) for t in range(self.child_rows)]
        self.second_start = [
            sum(1 for b in second if b[0] < t) for t in range(self.child_rows)
        ]

    def dest(self, block):
        high = quot(block, self.cols)
        return rem(block, self.cols), quot(high, self.slots), rem(high, self.slots)

    def offset(self, starts, t):
        out = jnp.int32(starts[0])
        for step in range(1, len(starts)):
            out = jnp.where(t == step, jnp.int32(starts[step]), out)
        return out


def take_rows(ref, lead, base, index, part, lanes):
    if part % 8 == 0:
        return ref[(*lead, pl.ds(pl.multiple_of(base + index * part, part), part), lanes)]
    share = 8 // part
    group = ref[(*lead, pl.ds(pl.multiple_of(base + quot(index, share) * 8, 8), 8), lanes)]
    out = group[:part]
    for step in range(1, share):
        out = jnp.where(rem(index, share) == step, group[step * part : (step + 1) * part], out)
    return out


def put_rows(ref, base, index, lanes, value):
    part = value.shape[0]
    if part % 8 == 0:
        ref[pl.ds(pl.multiple_of(base + index * part, part), part), lanes] = value
        return
    share = 8 // part
    rows = pl.ds(pl.multiple_of(base + quot(index, share) * 8, 8), 8)
    spot = lax.broadcasted_iota(jnp.int32, (8, value.shape[1]), 0)
    mine = quot(spot, part) == rem(index, share)
    ref[rows, lanes] = jnp.where(mine, jnp.concatenate([value] * share, axis=0), ref[rows, lanes])


def block_lanes(number):
    return slice(number * BLK, (number + 1) * BLK)


def cut_child_kernel(plan, tile_ref, out_ref):
    for k in range(plan.plane):
        for b, (t, u) in enumerate(plan.blocks[: plan.first]):
            rows = slice(t * BLK + k * plan.part, t * BLK + (k + 1) * plan.part)
            out_ref[k, b] = tile_ref[0, rows, block_lanes(u)]


def cut_rest_kernel(plan, tile_ref, front_ref, map_ref, out_ref):
    for k in range(plan.plane):
        for b, (t, u) in enumerate(plan.blocks[plan.first :]):
            rows = slice(t * BLK + k * plan.part, t * BLK + (k + 1) * plan.part)
            out_ref[k, b] = tile_ref[0, rows, block_lanes(u)]
        out_ref[k, plan.rest - 1] = map_ref[...]

    @pl.loop(0, plan.row_blocks)
    def _(t):
        for k in range(plan.plane):
            for u in range(plan.lead_cols):
                out_ref[k, plan.second + t * plan.lead_cols + u] = take_rows(
                    front_ref, (), t * BLK, jnp.int32(k), plan.part, block_lanes(u)
                )


def front_panel_kernel(plan, pieces_ref, panel_ref, lead_ref):
    for pivot in range(NPIV):
        owner = pivot % plan.cols * plan.subs

        @pl.loop(0, plan.row_blocks)
        def _(t):
            panel_ref[t, pivot] = pieces_ref[
                owner, plan.second + t * plan.lead_cols + pivot // plan.cols
            ]

    for r in range(plan.rows):
        lead_ref[r] = panel_ref[: plan.lead_rows]


def pack(block, pivot):
    return (block * (block + 1)) // 2 + pivot


def ring_copies(plan, pieces, held, first_block, count, sems, first_sem):
    copies = []
    for number, (h, low, high, piece) in enumerate(pieces):
        copies.append(
            pltpu.make_async_copy(
                piece,
                held.at[h, pl.ds(low, high - low), pl.ds(first_block, count)],
                sems.at[first_sem + number],
            )
        )
    return copies


def panel_kernel(plan, spans, place_ref, maps_ref, *refs):
    rows = plan.rows
    ring = refs[: len(spans)]
    front_ref, panel_ref, corner_ref, across, held, sems = refs[len(spans) :]
    row, col, sub = place_ref[1], place_ref[2], place_ref[3]
    copies = ring_copies(
        plan, [(*span, piece) for span, piece in zip(spans, ring)], held, 0, plan.first, sems, 0
    )
    for copy in copies:
        copy.start()
    panel_ref[...] = front_ref[...]
    corner_ref[...] = jnp.zeros_like(corner_ref)
    across[...] = jnp.zeros_like(across)
    for copy in copies:
        copy.wait()

    def place(block):
        block_col, block_sub, slot = plan.dest(block)
        return block_col * plan.subs + block_sub, slot

    @pl.loop(0, plan.subs)
    def _(ms):
        @pl.loop(0, min(NPIV, plan.order))
        def _(j):
            pivot = maps_ref[ms, j]

            @pl.when(pivot < NPIV)
            def _():
                u = quot(j, plan.cols)
                m = rem(j, plan.cols) * plan.subs + ms

                @pl.loop(j, plan.order)
                def _(i):
                    block = maps_ref[ms, i]
                    h = rem(row - rem(i, rows) + rows, rows)
                    b = plan.offset(plan.first_start, quot(i, rows)) + u

                    @pl.when(rem(block, rows) == row)
                    def _():
                        panel_ref[quot(block, rows), pivot] += held[h, m, b]

                    @pl.when(block < NPIV)
                    def _():
                        base = lax.shift_right_logical(block * (block + 1), jnp.int32(1))
                        corner_ref[base + pivot] += held[h, m, b]

                    @pl.when(rem(pivot, rows) == row)
                    def _():
                        target, slot = place(block)
                        across[target, quot(pivot, rows), slot] += held[h, m, b]

                    @pl.when((block < NPIV) & (block != pivot) & (rem(block, rows) == row))
                    def _():
                        target, slot = place(pivot)
                        across[target, quot(block, rows), slot] += held[h, m, b]


def corner_front_kernel(plan, part_ref, leads_ref, out_ref):
    for block in range(NPIV):
        for pivot in range(block + 1):
            spot = pack(block, pivot)
            out_ref[spot] = (
                part_ref[spot] + leads_ref[block % plan.rows, block // plan.rows, pivot]
            )


def spread_kernel(plan, spans, one_way, place_ref, maps_ref, table_ref, more_ref, *refs):
    rows, plane = plan.rows, plan.plane
    count = len(spans)
    total_count = count + len(one_way)
    ring_first, ring_second = refs[:count], refs[count:total_count]
    outs, rests, held, total, sems, out_sems, rest_sems = refs[total_count:]
    me, row, col, sub = place_ref[0], place_ref[1], place_ref[2], place_ref[3]
    copies = ring_copies(
        plan, [(*span, piece) for span, piece in zip(spans, ring_first)], held, 0, plan.first,
        sems, 0,
    ) + ring_copies(
        plan, [(*span, piece) for span, piece in zip(one_way, ring_second)], held, plan.first,
        plan.second, sems, count,
    )
    for copy in copies:
        copy.start()

    @pl.loop(0, plane)
    def _(m):
        chunk = 8

        @pl.loop(0, plan.limit // chunk)
        def _(step):
            total[m, pl.ds(step * chunk, chunk)] = jnp.zeros((chunk, plan.part, BLK), jnp.float32)

        @pl.when(more_ref[0] > 0)
        def _():
            @pl.loop(plan.limit // chunk, plan.area // chunk)
            def _(step):
                total[m, pl.ds(step * chunk, chunk)] = jnp.zeros(
                    (chunk, plan.part, BLK), jnp.float32
                )

    for copy in copies:
        copy.wait()

    @pl.loop(0, plan.subs)
    def _(ms):
        @pl.loop(0, plan.order)
        def _(i):
            block_row = maps_ref[ms, i]

            @pl.when((rem(block_row, rows) == row) & (block_row >= NPIV))
            def _():
                line = quot(block_row, rows) * plan.slots

                @pl.loop(0, plan.order)
                def _(j):
                    block = maps_ref[ms, j]

                    @pl.when(block >= NPIV)
                    def _():
                        block_col, block_sub, slot = plan.dest(block)
                        high = jnp.maximum(i, j)
                        low = jnp.minimum(i, j)
                        h = rem(row - rem(high, rows) + rows, rows)
                        t = quot(high, rows)
                        u = quot(low, plan.cols)
                        m = rem(low, plan.cols) * plan.subs + ms
                        b = jnp.where(
                            u < plan.lead_cols,
                            plan.offset(plan.first_start, t) + u,
                            plan.first + plan.offset(plan.second_start, t) + u - plan.lead_cols,
                        )
                        dest = block_col * plan.subs + block_sub
                        spot = table_ref[dest, line + slot]
                        total[dest, spot] += held[h, m, b]

    out_copies = [
        pltpu.make_async_copy(total.at[m, pl.ds(0, plan.limit)], outs.at[m], out_sems.at[m])
        for m in range(plane)
    ]
    for copy in out_copies:
        copy.start()

    @pl.when(more_ref[0] > 0)
    def _():
        rest_copies = [
            pltpu.make_async_copy(
                total.at[m, pl.ds(plan.limit, plan.area - plan.limit)], rests.at[m], rest_sems.at[m]
            )
            for m in range(plane)
        ]
        for copy in rest_copies:
            copy.start()
        for copy in rest_copies:
            copy.wait()

    for copy in out_copies:
        copy.wait()


def lead_rows_kernel(plan, place_ref, front_ref, parts_ref, out_ref):
    row, col, sub = place_ref[1], place_ref[2], place_ref[3]
    for q in range(plan.lead_rows):
        block = plan.rows * q + row
        for slot in range(plan.slots):
            column = (sub * plan.slots + slot) * plan.cols + col
            joined = jnp.concatenate(
                [parts_ref[k, q, slot] for k in range(plan.plane)], axis=0
            )
            joined = jnp.where(column > block, joined.T, joined)
            out_ref[q, :, block_lanes(slot)] = (
                front_ref[q * BLK : (q + 1) * BLK, block_lanes(slot)] + joined
            )


def spread_lane(value, lane):
    return jnp.broadcast_to(value[:, lane : lane + 1], value.shape)


def spread_row(value, row):
    return jnp.broadcast_to(value[row : row + 1, :], value.shape)


def factor_block(matrix):
    group = 8
    count = BLK // group
    shape = (group, BLK)
    at_row = lax.broadcasted_iota(jnp.int32, shape, 0)
    at_lane = lax.broadcasted_iota(jnp.int32, shape, 1)
    left = [matrix[group * s : group * (s + 1), :] for s in range(count)]
    right = [jnp.where(at_lane == at_row + group * s, 1.0, 0.0) for s in range(count)]
    for s in range(count):
        cols = {
            t: [spread_lane(left[t], group * s + q) for q in range(group)] for t in range(s, count)
        }
        for o in range(group):
            inverse = 1.0 / spread_row(cols[s][o], o)
            scale = [spread_row(cols[s][q], o) * inverse for q in range(o + 1, group)]
            row_left = spread_row(left[s], o) * inverse
            row_right = spread_row(right[s], o) * inverse
            for t in range(s, count):
                col = cols[t][o]
                if t == s:
                    col = jnp.where(at_row > o, col, 0.0)
                for q in range(o + 1, group):
                    cols[t][q] = cols[t][q] - col * scale[q - o - 1]
                left[t] = left[t] - col * row_left
                right[t] = right[t] - col * row_right
    for s in range(count):
        pivots = jnp.sum(
            jnp.where(at_lane == at_row + group * s, left[s], 0.0), axis=1, keepdims=True
        )
        root = lax.rsqrt(pivots)
        root = root * (1.5 - 0.5 * pivots * root * root)
        left[s] = jnp.where(at_lane >= at_row + group * s, left[s] * root, 0.0)
        right[s] = right[s] * root
    return jnp.concatenate(left, axis=0), jnp.concatenate(right, axis=0)


def corner_load_kernel(plan, steps, place_ref, near_ref, far_ref, factor_ref, work):
    me = place_ref[0]
    for m in range(plan.plane):
        part = (near_ref, far_ref)[m % 2].at[m // 2]
        for block in range(NPIV):
            for pivot in range(block + 1):
                put_rows(
                    work, block * BLK, me ^ m, block_lanes(pivot), part[pack(block, pivot)]
                )
    for block in range(NPIV):
        for pivot in range(block):
            work[block_lanes(pivot), block_lanes(block)] = work[
                block_lanes(block), block_lanes(pivot)
            ].T
    factor_ref[...] = jnp.zeros_like(factor_ref)
    eliminate(steps, factor_ref, work)


def corner_rest_kernel(steps, factor_in, work_in, factor_ref, work):
    factor_ref[...] = factor_in[...]
    work[...] = work_in[...]
    eliminate(steps, factor_ref, work)


def eliminate(steps, factor_ref, work):
    exact = functools.partial(
        lax.dot_general, precision=highest, preferred_element_type=jnp.float32
    )

    @pl.loop(*steps)
    def _(pivot):
        here = pl.ds(pl.multiple_of(pivot * BLK, BLK), BLK)
        upper, inverse = factor_block(work[here, here])
        factor_ref[here, here] = upper.T
        work[here, :] = exact(inverse, work[here, :], (((1,), (0,)), ((), ())))
        work[here, here] = inverse

        @pl.loop(pivot + 1, NPIV)
        def _(block):
            there = pl.ds(pl.multiple_of(block * BLK, BLK), BLK)
            lower = work[here, there].T
            factor_ref[there, here] = lower
            work[there, here] = jnp.zeros((BLK, BLK), jnp.float32)
            work[there, :] -= exact(lower, work[here, :], (((1,), (0,)), ((), ())))

        @pl.loop(pivot + 1, NPIV)
        def _(block):
            there = pl.ds(pl.multiple_of(block * BLK, BLK), BLK)
            work[here, there] = jnp.zeros((BLK, BLK), jnp.float32)


def halves(value):
    high = value.astype(jnp.bfloat16)
    return high, (value - high.astype(jnp.float32)).astype(jnp.bfloat16)


def right_kernel(plan, spans, place_ref, inverse_ref, *refs):
    leads = refs[: len(spans)]
    high_ref, low_ref, stack = refs[len(spans) :]
    row = place_ref[1]
    for (h, low, high), lead in zip(spans, leads):
        for q in range(low // BLK, -(-high // BLK)):
            start, end = max(low, q * BLK), min(high, (q + 1) * BLK)
            block = plan.rows * q + rem(row - h + plan.rows, plan.rows)

            @pl.when(block < NPIV)
            def _():
                spot = pl.multiple_of(block * BLK + (start - q * BLK), 8)
                stack[pl.ds(spot, end - start), :] = lead[start - low : end - low]

    for pivot in range(NPIV):
        depth = (pivot + 1) * BLK
        value = jnp.dot(
            inverse_ref[pivot * BLK : depth, :depth], stack[:depth, :],
            precision=highest, preferred_element_type=jnp.float32,
        )
        high, low = halves(value)
        high_ref[pivot * BLK : depth, :] = high
        low_ref[pivot * BLK : depth, :] = low


def left_kernel(plan, tile_blocks, place_ref, inverse_ref, factor_ref, *refs):
    count = plan.plane
    parts = refs[:2]
    high_ref, low_ref, own_ref, panel, value_ref = refs[2:]
    me, row, col = place_ref[0], place_ref[1], place_ref[2]
    step = pl.program_id(0)
    for t in range(tile_blocks):
        for m in range(count):
            for pivot in range(NPIV):
                put_rows(panel, t * BLK, me ^ m, block_lanes(pivot), parts[m % 2][m // 2, t, pivot])
    for pivot in range(0, NPIV, 2):
        depth = min(pivot + 2, NPIV) * BLK
        value_ref[:, pivot * BLK : depth] = lax.dot_general(
            panel[:, :depth], inverse_ref[pivot * BLK : depth, :depth],
            (((1,), (1,)), ((), ())),
            precision=highest, preferred_element_type=jnp.float32,
        )
    high, low = halves(value_ref[...])
    high_ref[...] = high
    low_ref[...] = low
    for t in range(tile_blocks):
        block = plan.rows * (step * tile_blocks + t) + row
        for u in range(plan.lead_cols):
            pivot = jnp.minimum(plan.cols * u + col, NPIV - 1)
            lanes = pl.ds(pl.multiple_of(pivot * BLK, BLK), BLK)
            here = (slice(t * BLK, (t + 1) * BLK), block_lanes(u))
            own_ref[here] = value_ref[t * BLK : (t + 1) * BLK, lanes]

            @pl.when(block < NPIV)
            def _():
                own_ref[here] = factor_ref[
                    pl.ds(pl.multiple_of(block * BLK, BLK), BLK), lanes
                ]


def schur_kernel(plan, tile_blocks, place_ref, table_ref, more_ref, front_ref, high_ref, low_ref,
                 own_ref, right_high_ref, right_low_ref, parts, rests, out_ref, rest, sems):
    plane = plan.plane
    me, row, col, sub = place_ref[0], place_ref[1], place_ref[2], place_ref[3]
    step = pl.program_id(0)

    @pl.when((step == 0) & (more_ref[0] > 0))
    def _():
        copy = pltpu.make_async_copy(rests, rest, sems)
        copy.start()
        copy.wait()

    update = jnp.dot(high_ref[...], right_high_ref[...], preferred_element_type=jnp.float32)
    update += jnp.dot(high_ref[...], right_low_ref[...], preferred_element_type=jnp.float32)
    update += jnp.dot(low_ref[...], right_high_ref[...], preferred_element_type=jnp.float32)
    out_ref[...] = front_ref[...] - update
    for t in range(tile_blocks):
        line = step * tile_blocks + t
        block = plan.rows * line + row
        for slot in range(plan.slots):
            column = (sub * plan.slots + slot) * plan.cols + col
            here = (slice(t * BLK, (t + 1) * BLK), block_lanes(slot))
            spot = table_ref[me, line * plan.slots + slot]

            @pl.when(spot >= 0)
            def _():
                def add(ref, place):
                    joined = jnp.concatenate([ref[k, place] for k in range(plane)], axis=0)
                    out_ref[here] += jnp.where(column > block, joined.T, joined)

                @pl.when(spot < plan.limit)
                def _():
                    add(parts, spot)

                @pl.when(spot >= plan.limit)
                def _():
                    add(rest, spot - plan.limit)

            @pl.when((block < NPIV) & (column >= NPIV))
            def _():
                out_ref[here] = jnp.zeros((BLK, BLK), jnp.float32)

            if slot < plan.lead_cols:
                @pl.when(column < NPIV)
                def _():
                    out_ref[here] = own_ref[here]


def swap(value, plan, bit):
    return lax.ppermute(value, PLANE, [(k, k ^ bit) for k in range(plan.plane)])


def exchange(pieces, plan):
    return [pieces[0]] + [swap(pieces[m], plan, m) for m in range(1, plan.plane)]


def gather_direct(value, plan):
    return [value] + [swap(value, plan, m) for m in range(2, plan.plane, 2)]


def spread_over(value, axis, count):
    return lax.all_to_all(jnp.broadcast_to(value, (count, *value.shape)), axis, 0, 0)


def shift(value, plan, step):
    pairs = [(r, (r + step) % plan.rows) for r in range(plan.rows)]
    return lax.ppermute(value, "row", pairs)


def ring_gather(value, plan, *hold):
    count = value.shape[0]
    middle = count // 2
    out = [(0, 0, count, value)]
    before = behind = value
    for h in range(1, (plan.rows + 1) // 2):
        before, behind = shift(before, plan, 1), shift(behind, plan, -1)
        out += [(h, 0, count, before), (plan.rows - h, 0, count, behind)]
    if plan.rows % 2 == 0 and plan.rows > 1:
        before, behind = after((before, behind), *hold)
        h = plan.rows // 2
        out.append((h, 0, middle, shift(before[:middle], plan, 1)))
        out.append((h, middle, count, shift(behind[middle:], plan, -1)))
    return out


def after(values, *others):
    return lax.optimization_barrier((values, others))[0]


def cover_table(maps, row, plan):
    blocks = plan.row_blocks * plan.rows
    numbers = jnp.arange(blocks, dtype=jnp.int32)
    present = jnp.any(maps[:, :, None] == numbers, axis=1) & (numbers >= NPIV)
    lines = present.reshape(plan.subs, plan.row_blocks, plan.rows).transpose(0, 2, 1)
    columns = present.reshape(plan.subs, plan.subs, plan.slots, plan.cols).transpose(0, 3, 1, 2)
    columns = columns.reshape(plan.subs, plan.plane, plan.slots)
    cover = jnp.any(
        lines[:, :, None, :, None] & columns[:, None, :, None, :], axis=0
    ).reshape(plan.rows, plan.plane, plan.area)
    more = (jnp.max(jnp.sum(cover.astype(jnp.int32), axis=-1)) > plan.limit).astype(jnp.int32)
    mine = lax.dynamic_index_in_dim(cover, row, 0, keepdims=False)
    order = jnp.arange(plan.area, dtype=jnp.int32)
    before = (order[:, None] < order[None, :]).astype(jnp.float32)
    rank = jnp.dot(mine.astype(jnp.float32), before, precision=highest)
    return jnp.where(mine, rank.astype(jnp.int32), -1), more


def body(front_entries, child_blocks, child_map):
    plan = Plan(front_entries.shape, child_blocks.shape)
    f32 = jnp.float32
    row = lax.axis_index("row").astype(jnp.int32)
    col = lax.axis_index("col").astype(jnp.int32)
    sub = lax.axis_index("sub").astype(jnp.int32)
    place = jnp.stack([col * plan.subs + sub, row, col, sub])
    vmem, smem, hbm = whole(pltpu.VMEM), whole(pltpu.SMEM), whole(pl.ANY)
    part, plane, rows = plan.part, plan.plane, plan.rows

    def shape(*sizes, dtype=f32):
        return jax.ShapeDtypeStruct(sizes, dtype)

    lead_width = plan.lead_cols * BLK
    local_rows = front_entries.shape[0]
    cut_first = pl.pallas_call(
        functools.partial(cut_child_kernel, plan),
        out_shape=shape(plane, plan.first, part, BLK),
        in_specs=[vmem],
        out_specs=vmem,
        compiler_params=params(),
        name="cut_child",
        cost_estimate=cost(2),
    )(child_blocks)
    first = lax.all_to_all(cut_first, PLANE, 0, 0, tiled=True)
    ring_first = ring_gather(first, plan)
    spans = [span for *span, _ in ring_first]
    ring_first = [piece for *_, piece in ring_first]

    map_rows = jnp.broadcast_to(
        jnp.pad(child_map.astype(f32), ((0, 0), (0, BLK - plan.order))), (part, BLK)
    )
    cut_rest = pl.pallas_call(
        functools.partial(cut_rest_kernel, plan),
        grid=(1,),
        out_shape=shape(plane, plan.rest, part, BLK),
        in_specs=[
            pl.BlockSpec(child_blocks.shape, lambda g: (0, 0, 0)),
            pl.BlockSpec((local_rows, lead_width), lambda g: (0, 0)),
            pl.BlockSpec((part, BLK), lambda g: (0, 0)),
        ],
        out_specs=vmem,
        compiler_params=params(),
        name="cut_rest",
        cost_estimate=cost(6),
    )(child_blocks, front_entries, map_rows)
    rest = lax.all_to_all(after(cut_rest, first), PLANE, 0, 0, tiled=True)
    rest = after(rest, *ring_first[1:3])
    maps = rest[: plan.subs, plan.rest - 1, 0, : plan.order].astype(jnp.int32)
    table, more = cover_table(maps, row, plan)
    more_flag = more.reshape(1)

    front_panel, front_lead = pl.pallas_call(
        functools.partial(front_panel_kernel, plan),
        out_shape=[
            shape(plan.row_blocks, NPIV, part, BLK),
            shape(rows, plan.lead_rows, NPIV, part, BLK),
        ],
        in_specs=[vmem],
        out_specs=[vmem] * 2,
        compiler_params=params(),
        name="front_panel",
        cost_estimate=cost(4),
    )(rest)
    leads = lax.all_to_all(front_lead, "row", 0, 0, tiled=True)
    second = after(rest[:, : plan.second], leads, *ring_first[1:])
    ring_second = [piece for *_, piece in ring_gather(second, plan)]

    corner_count = NPIV * (NPIV + 1) // 2
    panel, corner_part, lead_parts = pl.pallas_call(
        functools.partial(panel_kernel, plan, spans),
        out_shape=[
            shape(plan.row_blocks, NPIV, part, BLK),
            shape(corner_count, part, BLK),
            shape(plane, plan.lead_rows, plan.slots, part, BLK),
        ],
        in_specs=[smem, smem] + [hbm] * len(spans) + [vmem],
        out_specs=[vmem] * 3,
        scratch_shapes=[
            pltpu.VMEM((rows, plane, plan.first, part, BLK), f32),
            pltpu.SemaphoreType.DMA((len(spans),)),
        ],
        compiler_params=params(),
        name="panel",
        cost_estimate=cost(6),
    )(place, maps, *ring_first, front_panel)

    lead_got = lax.all_to_all(lead_parts, PLANE, 0, 0, tiled=True)
    lead_rows = pl.pallas_call(
        functools.partial(lead_rows_kernel, plan),
        grid=(1,),
        out_shape=shape(plan.lead_rows, BLK, plan.slots * BLK),
        in_specs=[
            smem,
            pl.BlockSpec((plan.lead_rows * BLK, plan.slots * BLK), lambda g: (0, 0)),
            vmem,
        ],
        out_specs=vmem,
        compiler_params=params(),
        name="lead_rows",
        cost_estimate=cost(3),
    )(place, front_entries, lead_got)
    corner_part = pl.pallas_call(
        functools.partial(corner_front_kernel, plan),
        out_shape=shape(corner_count, part, BLK),
        in_specs=[vmem] * 2,
        out_specs=vmem,
        compiler_params=params(),
        name="corner_front",
        cost_estimate=cost(1),
    )(corner_part, leads)
    corner_near = jnp.stack(gather_direct(corner_part, plan))
    panel = after(panel, corner_near)
    corner_far = swap(corner_near, plan, 1)
    corner_near, corner_far = after((corner_near, corner_far), lead_rows, ring_second)
    square = shape(NPIV * BLK, NPIV * BLK)
    middle = NPIV // 2
    factor, inverse = pl.pallas_call(
        functools.partial(corner_load_kernel, plan, (0, middle)),
        out_shape=[square] * 2,
        in_specs=[smem] + [vmem] * 2,
        out_specs=[vmem] * 2,
        compiler_params=params(),
        name="corner_first",
        cost_estimate=cost(21),
    )(place, corner_near, corner_far)
    line_rows = after(lead_rows.reshape(-1, plan.slots * BLK), ring_second)
    lead_ring = [(0, 0, line_rows.shape[0], line_rows)]
    for h in range(1, rows):
        lead_ring.append((h, 0, line_rows.shape[0], shift(line_rows, plan, h)))
    lead_spans = [span for *span, _ in lead_ring]
    lead_ring = [piece for *_, piece in lead_ring]
    panel_near = [panel]
    bits = [m for m in range(2, plane, 2) if m & (m - 1) == 0]
    for bit in bits:
        panel_near.append(swap(panel, plan, bit))
    inverse = after(inverse, panel_near[1])
    factor, inverse = pl.pallas_call(
        functools.partial(corner_rest_kernel, (middle, NPIV)),
        out_shape=[square] * 2,
        in_specs=[vmem] * 2,
        out_specs=[vmem] * 2,
        compiler_params=params(),
        name="corner_rest",
        cost_estimate=cost(20),
    )(factor, inverse)

    rest_count = plan.area - plan.limit
    ring_second = after(ring_second, inverse)
    spread = pl.pallas_call(
        functools.partial(spread_kernel, plan, spans, spans),
        out_shape=[
            shape(plane, plan.limit, part, BLK),
            shape(plane, rest_count, part, BLK),
        ],
        in_specs=[smem] * 4 + [hbm] * (2 * len(spans)),
        out_specs=[hbm] * 2,
        scratch_shapes=[
            pltpu.VMEM((rows, plane, plan.first + plan.second, part, BLK), f32),
            pltpu.VMEM((plane, plan.area, part, BLK), f32),
            pltpu.SemaphoreType.DMA((2 * len(spans),)),
            pltpu.SemaphoreType.DMA((plane,)),
            pltpu.SemaphoreType.DMA((plane,)),
        ],
        compiler_params=params(),
        name="spread",
        cost_estimate=cost(13),
    )(place, maps, table, more_flag, *ring_first, *ring_second)
    panel_held = {0: panel_near[0], **dict(zip(bits, panel_near[1:]))}
    for m in range(2, plane, 2):
        if m not in panel_held:
            low = m & -m
            panel_held[m] = swap(panel_held[m ^ low], plan, low)
    panel_near = jnp.stack([panel_held[m] for m in range(0, plane, 2)])
    panel_far = swap(after(panel_near, factor), plan, 1)
    right_high, right_low = pl.pallas_call(
        functools.partial(right_kernel, plan, lead_spans),
        out_shape=[shape(NPIV * BLK, plan.slots * BLK, dtype=jnp.bfloat16)] * 2,
        in_specs=[smem, vmem] + [vmem] * len(lead_spans),
        out_specs=[vmem] * 2,
        scratch_shapes=[pltpu.VMEM((NPIV * BLK, plan.slots * BLK), f32)],
        compiler_params=params(),
        name="right_factor",
        cost_estimate=cost(10),
    )(place, inverse, *lead_ring)

    tile = 2
    steps = plan.row_blocks // tile
    full = lambda g: (0, 0)
    by_row = lambda g: (g, 0)
    left_high, left_low, own = pl.pallas_call(
        functools.partial(left_kernel, plan, tile),
        grid=(steps,),
        out_shape=[
            shape(local_rows, NPIV * BLK, dtype=jnp.bfloat16),
            shape(local_rows, NPIV * BLK, dtype=jnp.bfloat16),
            shape(local_rows, lead_width),
        ],
        in_specs=[smem, vmem, vmem]
        + [
            pl.BlockSpec((plane // 2, tile, NPIV, part, BLK), lambda g: (0, g, 0, 0, 0))
        ]
        * 2,
        out_specs=[
            pl.BlockSpec((tile * BLK, NPIV * BLK), by_row),
            pl.BlockSpec((tile * BLK, NPIV * BLK), by_row),
            pl.BlockSpec((tile * BLK, lead_width), by_row),
        ],
        scratch_shapes=[
            pltpu.VMEM((tile * BLK, NPIV * BLK), f32),
            pltpu.VMEM((tile * BLK, NPIV * BLK), f32),
        ],
        compiler_params=params(),
        name="left_factor",
        cost_estimate=cost(18),
    )(place, inverse, factor, panel_near, panel_far)

    def trade(value):
        return lax.all_to_all(value, PLANE, 0, 0, tiled=True)

    spread_got = trade(after(spread[0], panel_near))
    rest_got = lax.cond(more > 0, trade, lambda value: value, spread[1])

    width = plan.slots * BLK
    return pl.pallas_call(
        functools.partial(schur_kernel, plan, tile),
        grid=(steps,),
        out_shape=jax.ShapeDtypeStruct(front_entries.shape, f32),
        in_specs=[smem] * 3
        + [
            pl.BlockSpec((tile * BLK, width), by_row),
            pl.BlockSpec((tile * BLK, NPIV * BLK), by_row),
            pl.BlockSpec((tile * BLK, NPIV * BLK), by_row),
            pl.BlockSpec((tile * BLK, lead_width), by_row),
            pl.BlockSpec((NPIV * BLK, width), full),
            pl.BlockSpec((NPIV * BLK, width), full),
            vmem,
            hbm,
        ],
        out_specs=pl.BlockSpec((tile * BLK, width), by_row),
        scratch_shapes=[
            pltpu.VMEM((plane, rest_count, part, BLK), f32),
            pltpu.SemaphoreType.DMA,
        ],
        compiler_params=params(),
        name="schur",
        cost_estimate=cost(20),
    )(
        place, table, more_flag, front_entries, left_high, left_low, own, right_high, right_low,
        spread_got, rest_got,
    )


def solution(mesh):
    placed = (P("row", ("col", "sub")), P("sub", "row", "col"), P("sub", None))
    return jax.shard_map(
        body, mesh=mesh, in_specs=placed, out_specs=P("row", ("col", "sub")), check_vma=False
    )
```
